32 devices in a mesh: batch: 2 (over y), fx: 4 (over z), fy: 4 (over x, core).
Axes of the slice: x: 2, y: 2, z: 4, core: 2. Of those that a mesh axis runs over, the one named last changes fastest.
Arguments:
- image_pool: bfloat16 [2, 4, 256, 6144], P('batch', None, None, 'fx'), may hold values from -6 to 6
- escalated: int32 [2, 2], P('batch'), may hold values from 0 to 3
- up_weight: bfloat16 [6144, 24576], P('fx', 'fy'), may hold values from -0.078125 to 0.078125
- down_weight: bfloat16 [24576, 6144], P('fy', 'fx'), may hold values from -0.0390625 to 0.0390625
- cotangent: bfloat16 [2, 2, 256, 6144], P('batch', None, None, 'fx'), may hold values from -6 to 6
Outputs:
- input_grad: bfloat16 [2, 2, 256, 6144], P('batch', None, None, 'fx')
- up_grad: bfloat16 [6144, 24576], P('fx', 'fy')
- down_grad: bfloat16 [24576, 6144], P('fy', 'fx')
The draws below stay inside these ranges and needn't reach their ends.
All inputs are finite; a program needn't handle non-finite values.
Results may differ from the reference program's by a relative error of at most 0.018.
Values may be sent and summed in bfloat16 or wider, within the bound.
A program may use at most 256 MiB of HBM per device.

```python
import jax
import jax.numpy as jnp
from jax import lax

D = 6144
FF = 24576
S = 256
IMG = 2
POOL = 4
REPLICAS = 2
N_BATCH = 2
N_FX = 4
N_FY = 4


def with_ends(entries, own_key, least, high):
    place = [jax.random.randint(jax.random.fold_in(own_key, axis), (), 0, length) for axis, length in enumerate(entries.shape)]
    longest = entries.shape.index(max(entries.shape))
    next_to = place[:longest] + [(place[longest] + 1) % entries.shape[longest]] + place[longest + 1:]
    return entries.at[tuple(place)].set(least).at[tuple(next_to)].set(high)


def level_of(own_key, extent, cuts, low, high):
    level = 1.0
    for dim, blocks in cuts:
        draws = jax.random.uniform(jax.random.fold_in(jax.random.fold_in(own_key, 6), dim), (blocks,), jnp.float32, low / len(cuts), high / len(cuts))
        level = level * jnp.repeat(jnp.exp(draws), extent[dim] // blocks).reshape((-1,) + (1,) * (len(extent) - 1 - dim))
    return level


def normal_values(rng, extent, deviation, limit, split=(), dtype=jnp.bfloat16):
    drawn = deviation * jax.random.normal(rng, extent, jnp.float32)
    if split:
        drawn = drawn * level_of(rng, extent, split, -0.22, 0.18)
    return jnp.clip(drawn, -limit, limit).astype(dtype)


def setup_inputs(seed: int = 0) -> dict:
    seeds = jax.random.split(jax.random.key(seed), 6)
    image_pool = normal_values(seeds[0], (REPLICAS, POOL, S, D), 1.0, 6.0, ((0, 2), (3, 4)))
    escalated = with_ends(jax.random.randint(seeds[1], (REPLICAS, IMG), 0, POOL), jax.random.fold_in(seeds[1], 1), 0, POOL - 1).astype(jnp.int32)
    up_weight = normal_values(seeds[2], (D, FF), D ** -0.5, 0.078125, ((0, 4), (1, 4)))
    down_weight = normal_values(seeds[3], (FF, D), FF ** -0.5, 0.0390625, ((0, 4), (1, 4)))
    cotangent = normal_values(seeds[4], (REPLICAS, IMG, S, D), 1.0, 6.0, ((0, 2), (3, 4)))
    return dict(image_pool=image_pool, escalated=escalated, up_weight=up_weight, down_weight=down_weight, cotangent=cotangent)


root_half = 0.7071067811865476
inv_root_tau = 0.3989422804014327


def rounded(value):
    return lax.optimization_barrier(value.astype(jnp.bfloat16)).astype(jnp.float32)


def gelu_value(pre_act):
    return 0.5 * pre_act * (1.0 + lax.erf(pre_act * root_half))


def gelu_slope(pre_act):
    return 0.5 * (1.0 + lax.erf(pre_act * root_half)) + pre_act * jnp.exp(-0.5 * pre_act * pre_act) * inv_root_tau


def reference(image_pool, escalated, up_weight, down_weight, cotangent):
    model_width = up_weight.shape[0]
    hidden = up_weight.shape[1]
    fx_width = model_width // N_FX
    fy_width = hidden // N_FY
    up_total = jnp.zeros((model_width, hidden), jnp.float32)
    down_total = jnp.zeros((hidden, model_width), jnp.float32)
    input_rows = []
    for replica in range(N_BATCH):
        inputs = jnp.take(image_pool[replica], escalated[replica], axis=0).reshape(-1, model_width)
        upstream = cotangent[replica].reshape(-1, model_width)
        pre_act = jnp.zeros((inputs.shape[0], hidden), jnp.float32)
        grad_act = jnp.zeros((inputs.shape[0], hidden), jnp.float32)
        for fx_index in range(N_FX):
            offset = fx_index * fx_width
            pre_act = pre_act + rounded(jnp.dot(inputs[:, offset:offset + fx_width], up_weight[offset:offset + fx_width, :], preferred_element_type=jnp.float32))
            grad_act = grad_act + rounded(jnp.dot(upstream[:, offset:offset + fx_width], down_weight[:, offset:offset + fx_width].T, preferred_element_type=jnp.float32))
        act_rows = gelu_value(pre_act).astype(jnp.bfloat16)
        grad_rows = (grad_act * gelu_slope(pre_act)).astype(jnp.bfloat16)
        down_total = down_total + rounded(jnp.dot(act_rows.T, upstream, preferred_element_type=jnp.float32))
        up_total = up_total + rounded(jnp.dot(inputs.T, grad_rows, preferred_element_type=jnp.float32))
        input_total = jnp.zeros((inputs.shape[0], model_width), jnp.float32)
        for fy_index in range(N_FY):
            offset = fy_index * fy_width
            input_total = input_total + rounded(jnp.dot(grad_rows[:, offset:offset + fy_width], up_weight[:, offset:offset + fy_width].T, preferred_element_type=jnp.float32))
        input_rows.append(input_total.astype(jnp.bfloat16).reshape(cotangent.shape[1:]))
    return jnp.stack(input_rows), up_total.astype(jnp.bfloat16), down_total.astype(jnp.bfloat16)
```

```python
import jax
import jax.numpy as jnp
from jax import lax
from jax.sharding import PartitionSpec as P

root_half = 0.7071067811865476
inv_root_tau = 0.3989422804014327
CHUNKS = 12


def gelu_value(pre_act):
    return 0.5 * pre_act * (1.0 + lax.erf(pre_act * root_half))


def gelu_slope(pre_act):
    return (
        0.5 * (1.0 + lax.erf(pre_act * root_half))
        + pre_act * jnp.exp(-0.5 * pre_act * pre_act) * inv_root_tau
    )


def contract_rows(left, right):
    return lax.dot_general(
        left, right, (((0,), (0,)), ((), ())), preferred_element_type=jnp.float32
    )


def contract_last(left, right):
    return lax.dot_general(
        left, right, (((1,), (1,)), ((), ())), preferred_element_type=jnp.float32
    )


def swap_batch(value, n_batch):
    return [
        lax.ppermute(value, "batch", [(i, (i + step) % n_batch) for i in range(n_batch)])
        for step in range(1, n_batch)
    ]


def make_per_device(n_batch, n_fx, chunks):
    half = n_fx // 2
    middle = [(half - 1, half), (half, half - 1)]

    def inward(step):
        return [(step, step + 1), (n_fx - 1 - step, n_fx - 2 - step)]

    def outward(step):
        return [(step + 1, step), (n_fx - 2 - step, n_fx - 1 - step)]

    def per_device(image_pool, escalated, up_weight, down_weight, cotangent):
        fx_width = image_pool.shape[3]
        place = lax.axis_index("fx")
        on_left = place < half
        chosen = jnp.take(image_pool[0], escalated[0], axis=0)
        inputs = chosen.reshape(-1, fx_width)
        upstream = cotangent.reshape(-1, fx_width)
        rows = inputs.shape[0]
        hidden = up_weight.shape[1]
        width = hidden // chunks

        own = jnp.stack([inputs, upstream])
        all_pairs = jnp.concatenate([own] + swap_batch(own, n_batch), axis=1)

        state = dict(
            last=None,
            sums=(
                jnp.zeros((rows, fx_width), jnp.float32),
                jnp.zeros(up_weight.shape, jnp.bfloat16),
                jnp.zeros(down_weight.shape, jnp.bfloat16),
            ),
        )

        def in_order(*values):
            if state["last"] is None:
                return values
            return lax.optimization_barrier((state["last"],) + values)[1:]

        def first_products(chunk):
            first = chunk * width
            left, right = in_order(inputs, upstream)
            part = jnp.stack([
                jnp.dot(
                    left, up_weight[:, first:first + width], preferred_element_type=jnp.float32
                ).astype(jnp.bfloat16),
                contract_last(right, down_weight[first:first + width, :]).astype(jnp.bfloat16),
            ])
            state["last"] = part
            return part

        def fold(step):
            def work(held):
                part, arrived = in_order(*held)
                part = part + arrived
                state["last"] = part
                return part

            return work

        def send_inward(step):
            return lambda part: (part, lax.ppermute(part, "fx", inward(step)))

        def send_half(part):
            low, high = part[:, :rows // 2], part[:, rows // 2:]
            kept = jnp.where(on_left, low, high)
            given = jnp.where(on_left, high, low)
            state["last"] = given
            return kept, lax.ppermute(given, "fx", middle)

        def activate(held):
            kept, arrived = in_order(*held)
            total = kept.astype(jnp.float32) + arrived.astype(jnp.float32)
            pre_act, grad_act = total[0], total[1]
            share = jnp.stack([
                gelu_value(pre_act).astype(jnp.bfloat16),
                (grad_act * gelu_slope(pre_act)).astype(jnp.bfloat16),
            ])
            state["last"] = share
            return share

        def send_share(share):
            return share, lax.ppermute(share, "fx", middle)

        def join(held):
            share, other = in_order(*held)
            full = jnp.concatenate(
                [jnp.where(on_left, share, other), jnp.where(on_left, other, share)], axis=1
            )
            state["last"] = full
            return full

        def send_outward(step):
            return lambda full: (full, lax.ppermute(full, "fx", outward(step)))

        def spread(step):
            def work(held):
                full, arrived = in_order(*held)
                takes = (place == step) | (place == n_fx - 1 - step)
                full = jnp.where(takes, arrived, full)
                state["last"] = full
                return full

            return work

        def send_replica(full):
            return [full] + swap_batch(full, n_batch)

        def last_products(chunk, held):
            first = chunk * width
            inp_sum, up_sum, down_sum = state["sums"]
            *held, pairs, inp_sum, up_sum, down_sum = in_order(
                *held, all_pairs, inp_sum, up_sum, down_sum
            )
            everyone = jnp.concatenate(held, axis=1)
            inp_sum = inp_sum + contract_last(held[0][1], up_weight[:, first:first + width])
            up_sum = lax.dynamic_update_slice(
                up_sum, contract_rows(pairs[0], everyone[1]).astype(jnp.bfloat16), (0, first)
            )
            down_sum = lax.dynamic_update_slice(
                down_sum, contract_rows(everyone[0], pairs[1]).astype(jnp.bfloat16), (first, 0)
            )
            state["sums"] = lax.optimization_barrier((inp_sum, up_sum, down_sum))
            state["last"] = state["sums"][0]

        works = [fold(step) for step in range(half - 1)] + [activate, join]
        works += [spread(step) for step in reversed(range(half - 1))]
        sends = [send_inward(step) for step in range(half - 1)] + [send_half, send_share]
        sends += [send_outward(step) for step in reversed(range(half - 1))] + [send_replica]
        depth = len(sends)
        held = {}
        for tick in range(chunks + depth):
            if tick < chunks:
                held[tick] = sends[0](first_products(tick))
            for stage, work in enumerate(works, 1):
                chunk = tick - stage
                if 0 <= chunk < chunks:
                    held[chunk] = sends[stage](work(held[chunk]))
            chunk = tick - depth
            if 0 <= chunk < chunks:
                last_products(chunk, held.pop(chunk))
        input_part, up_total, down_total = state["sums"]
        input_total = lax.psum(input_part.astype(jnp.bfloat16), "fy")
        return (input_total.reshape(cotangent.shape), up_total, down_total)

    return per_device


def solution(mesh):
    placed = (
        P("batch", None, None, "fx"),
        P("batch", None),
        P("fx", "fy"),
        P("fy", "fx"),
        P("batch", None, None, "fx"),
    )
    return jax.shard_map(
        make_per_device(mesh.shape["batch"], mesh.shape["fx"], CHUNKS),
        mesh=mesh,
        in_specs=placed,
        out_specs=(P("batch", None, None, "fx"), P("fx", "fy"), P("fy", "fx")),
        check_vma=False,
    )
```

```python
import jax
import jax.numpy as jnp
from jax import lax
from jax.sharding import PartitionSpec as P

root_half = 0.7071067811865476
inv_root_tau = 0.3989422804014327
CHUNKS = 12


def gelu_value(pre_act):
    return 0.5 * pre_act * (1.0 + lax.erf(pre_act * root_half))


def gelu_slope(pre_act):
    return (
        0.5 * (1.0 + lax.erf(pre_act * root_half))
        + pre_act * jnp.exp(-0.5 * pre_act * pre_act) * inv_root_tau
    )


def contract_rows(left, right):
    return lax.dot_general(
        left, right, (((0,), (0,)), ((), ())), preferred_element_type=jnp.float32
    )


def contract_last(left, right):
    return lax.dot_general(
        left, right, (((1,), (1,)), ((), ())), preferred_element_type=jnp.float32
    )


def swap_batch(value, n_batch):
    return [
        lax.ppermute(value, "batch", [(i, (i + step) % n_batch) for i in range(n_batch)])
        for step in range(1, n_batch)
    ]


def make_per_device(n_batch, n_fx, chunks):
    half = n_fx // 2
    middle = [(half - 1, half), (half, half - 1)]

    def inward(step):
        return [(step, step + 1), (n_fx - 1 - step, n_fx - 2 - step)]

    def outward(step):
        return [(step + 1, step), (n_fx - 2 - step, n_fx - 1 - step)]

    def per_device(image_pool, escalated, up_weight, down_weight, cotangent):
        fx_width = image_pool.shape[3]
        place = lax.axis_index("fx")
        on_left = place < half
        chosen = jnp.take(image_pool[0], escalated[0], axis=0)
        inputs = chosen.reshape(-1, fx_width)
        upstream = cotangent.reshape(-1, fx_width)
        rows = inputs.shape[0]
        share_rows = rows // 2

        def turned(value):
            return jnp.where(on_left, value, jnp.roll(value, share_rows, axis=0))

        inputs, upstream = turned(inputs), turned(upstream)
        hidden = up_weight.shape[1]
        width = hidden // chunks

        own = jnp.stack([inputs, upstream])
        all_pairs = jnp.concatenate([own] + swap_batch(own, n_batch), axis=1)

        state = dict(
            last=None,
            input=jnp.zeros((rows, fx_width), jnp.float32),
            sums=(
                jnp.zeros(up_weight.shape, jnp.bfloat16),
                jnp.zeros(down_weight.shape, jnp.bfloat16),
            ),
        )

        def in_order(*values):
            if state["last"] is None:
                return values
            return lax.optimization_barrier((state["last"],) + values)[1:]

        def first_products(chunk):
            first = chunk * width
            left, right = in_order(inputs, upstream)
            part = jnp.stack([
                jnp.dot(
                    left, up_weight[:, first:first + width], preferred_element_type=jnp.float32
                ).astype(jnp.bfloat16),
                contract_last(right, down_weight[first:first + width, :]).astype(jnp.bfloat16),
            ])
            state["last"] = part
            return part

        def fold(step):
            def work(held):
                part, arrived = in_order(*held)
                part = part + arrived
                state["last"] = part
                return part

            return work

        def send_inward(step):
            return lambda part: (part, lax.ppermute(part, "fx", inward(step)))

        def fold_given(held):
            part, arrived = in_order(*held)
            given = part[:, share_rows:] + arrived[:, share_rows:]
            state["last"] = given
            return part, arrived, given

        def send_half(held):
            part, arrived, given = held
            return part, arrived, lax.ppermute(given, "fx", middle)

        def activate(held):
            part, arrived, other = in_order(*held)
            total = (
                part[:, :share_rows].astype(jnp.float32)
                + arrived[:, :share_rows].astype(jnp.float32)
                + other.astype(jnp.float32)
            )
            pre_act, grad_act = total[0], total[1]
            share = jnp.stack([
                gelu_value(pre_act).astype(jnp.bfloat16),
                (grad_act * gelu_slope(pre_act)).astype(jnp.bfloat16),
            ])
            state["last"] = share
            return share

        def send_share(share):
            return share, lax.ppermute(share, "fx", middle)

        def join(held):
            share, other = in_order(*held)
            full = jnp.concatenate([share, other], axis=1)
            state["last"] = full
            return full

        def send_outward(step):
            return lambda full: (full, lax.ppermute(full, "fx", outward(step)))

        def spread(step):
            def work(held):
                full, arrived = in_order(*held)
                takes = (place == step) | (place == n_fx - 1 - step)
                full = jnp.where(takes, arrived, full)
                state["last"] = full
                return full

            return work

        def send_replica(full):
            return [full] + swap_batch(full, n_batch)

        def input_product(chunk, full):
            first = chunk * width
            full, total = in_order(full, state["input"])
            total = total + contract_last(full[1], up_weight[:, first:first + width])
            state["input"] = total
            if chunk == chunks - 1:
                total = turned(total).astype(jnp.bfloat16)
                state["input"] = lax.psum(total, "fy")
            state["last"] = total

        def last_products(chunk, held):
            first = chunk * width
            *held, pairs, up_sum, down_sum = in_order(*held, all_pairs, *state["sums"])
            everyone = jnp.concatenate(held, axis=1)
            up_sum = lax.dynamic_update_slice(
                up_sum, contract_rows(pairs[0], everyone[1]).astype(jnp.bfloat16), (0, first)
            )
            down_sum = lax.dynamic_update_slice(
                down_sum, contract_rows(everyone[0], pairs[1]).astype(jnp.bfloat16), (first, 0)
            )
            state["sums"] = lax.optimization_barrier((up_sum, down_sum))
            state["last"] = state["sums"]

        works = [fold(step) for step in range(half - 2)] + [fold_given, activate, join]
        works += [spread(step) for step in reversed(range(half - 1))]
        sends = [send_inward(step) for step in range(half - 1)] + [send_half, send_share]
        sends += [send_outward(step) for step in reversed(range(half - 1))] + [send_replica]
        depth = len(sends)
        held = {}
        for tick in range(chunks + depth):
            if tick < chunks:
                held[tick] = sends[0](first_products(tick))
            for stage, work in enumerate(works, 1):
                chunk = tick - stage
                if 0 <= chunk < chunks:
                    done = work(held[chunk])
                    held[chunk] = sends[stage](done)
                    if stage == depth - 1:
                        input_product(chunk, done)
            chunk = tick - depth
            if 0 <= chunk < chunks:
                last_products(chunk, held.pop(chunk))
        up_total, down_total = state["sums"]
        return (state["input"].reshape(cotangent.shape), up_total, down_total)

    return per_device


def solution(mesh):
    placed = (
        P("batch", None, None, "fx"),
        P("batch", None),
        P("fx", "fy"),
        P("fy", "fx"),
        P("batch", None, None, "fx"),
    )
    return jax.shard_map(
        make_per_device(mesh.shape["batch"], mesh.shape["fx"], CHUNKS),
        mesh=mesh,
        in_specs=placed,
        out_specs=(P("batch", None, None, "fx"), P("fx", "fy"), P("fy", "fx")),
        check_vma=False,
    )
```
